1024 devices in a mesh: dp: 128 (over z, x, core), tensor: 8 (over y).
Axes of the slice: x: 8, y: 8, z: 8, core: 2. Of those that a mesh axis runs over, the one named last changes fastest.
Arguments:
- tokens: bfloat16 [16384, 8192], P(('dp', 'tensor')), may hold values from -6 to 6
- grad_out: bfloat16 [16384, 28672], P('dp', 'tensor'), may hold values from -0.046875 to 0.046875
- basis: bfloat16 [8192, 128], replicated, may hold values from -0.0625 to 0.0625
- weight: float32 [8192, 28672], P('dp', 'tensor'), may hold values from -0.75 to 0.75
- exp_avg: float32 [128, 28672], P('dp', 'tensor'), may hold values from -4 to 4
- exp_avg_sq: float32 [128, 28672], P('dp', 'tensor'), may hold values from 0.0001 to 0.01
Outputs:
- new_weight: float32 [8192, 28672], P('dp', 'tensor')
- new_avg: float32 [128, 28672], P('dp', 'tensor')
- new_avg_sq: float32 [128, 28672], P('dp', 'tensor')
The draws below stay inside these ranges and needn't reach their ends.
All inputs are finite; a program needn't handle non-finite values.
Results may differ from the reference program's by a relative error of at most 0.0033.
Values may be sent and summed in bfloat16 or wider, within the bound.
No kernel may reach another device: no remote copies, remote signals or barrier semaphores. Data moves between devices by JAX's collectives and lax.ppermute only.
A program may use at most 32 MiB of HBM per device.

```python
import math
import jax
import jax.numpy as jnp

D = 8192
FF = 28672
RANK = 128
STEP = 10
TOKENS = 16384


def block_levels(stream_key, extent, shards, least, high):
    def one(dim, shards_of):
        steps = jax.random.uniform(jax.random.fold_in(jax.random.fold_in(stream_key, 6), dim), (shards_of,), jnp.float32, least / len(shards), high / len(shards))
        return jnp.repeat(jnp.exp(steps), extent[dim] // shards_of).reshape((-1,) + (1,) * (len(extent) - dim - 1))

    loudness = one(*shards[0])
    for cut in shards[1:]:
        loudness = loudness * one(*cut)
    return loudness


def noise(stream_key, shape, scale, reach, shards=(), kind=jnp.bfloat16):
    result = jax.random.normal(stream_key, shape, jnp.float32) * scale
    if len(shards) > 0:
        result = block_levels(stream_key, shape, shards, -0.22, 0.18) * result
    return jnp.clip(result, min=-reach, max=reach).astype(kind)


def setup_inputs(seed: int = 0) -> dict:
    arg_keys = jax.random.split(jax.random.key(seed), 7)
    return {
        "tokens": noise(arg_keys[0], (TOKENS, D), 1.0, 6.0, ((0, 1024),)),
        "grad_out": noise(arg_keys[1], (TOKENS, FF), TOKENS ** -0.5, 0.046875, ((0, 128), (1, 8))),
        "basis": noise(arg_keys[2], (D, RANK), D ** -0.5, 0.0625),
        "weight": noise(arg_keys[3], (D, FF), 0.05, 0.75, ((0, 128), (1, 8)), jnp.float32),
        "exp_avg": noise(arg_keys[4], (RANK, FF), 0.3, 4.0, ((0, 128), (1, 8)), jnp.float32),
        "exp_avg_sq": jnp.clip(jnp.exp(math.log(0.01) - 4.6051702 * jax.random.uniform(arg_keys[5], (RANK, FF), jnp.float32) ** block_levels(arg_keys[5], (RANK, FF), ((0, 128), (1, 8)), -0.2, 0.2)), 0.0001, 0.01),
    }


def reference(tokens, grad_out, basis, weight, exp_avg, exp_avg_sq):
    projected = jnp.dot(tokens.astype(jnp.float32), basis.astype(jnp.float32), preferred_element_type=jnp.float32).astype(jnp.bfloat16)
    reduced = jnp.dot(projected.astype(jnp.float32).T, grad_out.astype(jnp.float32), preferred_element_type=jnp.float32)
    new_avg = 0.9 * exp_avg + 0.1 * reduced
    new_avg_sq = 0.999 * exp_avg_sq + 0.001 * reduced * reduced
    first_fix = 1.0 - 0.9 ** STEP
    second_fix = 1.0 - 0.999 ** STEP
    direction = (new_avg / first_fix / (jnp.sqrt(new_avg_sq / second_fix) + 1e-08)).astype(jnp.bfloat16)
    delta = jnp.dot(basis.astype(jnp.float32), direction.astype(jnp.float32), preferred_element_type=jnp.float32)
    new_weight = weight - 0.5 * delta
    return (new_weight, new_avg, new_avg_sq)
```

```python
import jax
import jax.numpy as jnp
from jax import lax
from jax.sharding import Mesh
from jax.sharding import PartitionSpec as P

STEP = 10
CHIPS = ("z", "x")


def own_half_first(rank):
    core = lax.axis_index("core")
    row = lax.broadcasted_iota(jnp.int32, (rank, rank), 0)
    column = lax.broadcasted_iota(jnp.int32, (rank, rank), 1)
    half = rank // 2
    wanted = jnp.where(column < half, 2 * column + core, 2 * (column - half) + 1 - core)
    return (row == wanted).astype(jnp.bfloat16)


def other_core(value):
    return lax.ppermute(value, "core", [(0, 1), (1, 0)])


def body(tokens, grad_out, basis, weight, exp_avg, exp_avg_sq):
    f32, bf16 = jnp.float32, jnp.bfloat16
    rank, columns = basis.shape[1], grad_out.shape[1]
    half, lanes = rank // 2, 128
    groups = columns // lanes
    tensor = lax.axis_size("tensor")
    own_rows = tokens.shape[0]

    order = own_half_first(rank)
    projected = jnp.dot(tokens, basis, preferred_element_type=f32).astype(bf16)
    projected = jnp.dot(projected, order, preferred_element_type=f32).astype(bf16)
    projected = lax.all_to_all(
        jnp.broadcast_to(projected[None], (tensor, own_rows, rank)), "tensor", 0, 0, tiled=True
    ).reshape(tensor * own_rows, rank)
    partial = lax.dot_general(
        projected, grad_out, (((0,), (0,)), ((), ())), preferred_element_type=f32
    )
    received = other_core(partial[half:].astype(bf16))
    chip_sum = (partial[:half] + received.astype(f32)).astype(bf16)
    rows = lax.all_to_all(chip_sum.reshape(half, groups, lanes), CHIPS, 0, 0, tiled=True)
    reduced = jnp.sum(rows.astype(f32), axis=0).reshape(1, columns)

    new_avg = 0.9 * exp_avg + 0.1 * reduced
    new_avg_sq = 0.999 * exp_avg_sq + 0.001 * reduced * reduced
    first_fix = 1.0 - 0.9**STEP
    second_fix = 1.0 - 0.999**STEP
    direction = (new_avg / first_fix / (jnp.sqrt(new_avg_sq / second_fix) + 1e-08)).astype(bf16)

    own_core = lax.all_to_all(
        jnp.broadcast_to(direction.reshape(1, groups, lanes), (half, groups, lanes)),
        CHIPS, 0, 0, tiled=True,
    )
    other = other_core(own_core).reshape(half, columns)
    own_core = own_core.reshape(half, columns)
    weight_rows = weight.shape[0]
    owner = lax.axis_index(("z", "x", "core"))
    basis_rows = lax.dynamic_slice_in_dim(basis, owner * weight_rows, weight_rows, 0)
    basis_rows = jnp.dot(basis_rows, order, preferred_element_type=f32).astype(bf16)
    delta = jnp.dot(basis_rows[:, :half], own_core, preferred_element_type=f32)
    delta = delta + jnp.dot(basis_rows[:, half:], other, preferred_element_type=f32)
    return (weight - 0.5 * delta, new_avg, new_avg_sq)


def solution(mesh):
    split = Mesh(mesh.devices.reshape(8, 8, 2, 8), ("z", "x", "core", "tensor"))
    owners = ("z", "x", "core")
    shared = P(owners, "tensor")
    placed = (P(owners + ("tensor",), None), shared, P(), shared, shared, shared)
    return jax.shard_map(
        body, mesh=split, in_specs=placed, out_specs=(shared, shared, shared), check_vma=False
    )
```

```python
import jax
import jax.numpy as jnp
from jax import lax
from jax.sharding import Mesh
from jax.sharding import PartitionSpec as P

STEP = 10
CHIPS = ("z", "x")


def by_core(rank):
    row = lax.broadcasted_iota(jnp.int32, (rank, rank), 0)
    column = lax.broadcasted_iota(jnp.int32, (rank, rank), 1)
    half = rank // 2
    wanted = jnp.where(column < half, 2 * column, 2 * (column - half) + 1)
    return (row == wanted).astype(jnp.bfloat16)


def body(tokens, grad_out, basis, weight, exp_avg, exp_avg_sq):
    f32, bf16 = jnp.float32, jnp.bfloat16
    rank, columns = basis.shape[1], grad_out.shape[1]
    half = rank // 2
    piece = (4, columns // 4)
    tensor = lax.axis_size("tensor")
    own_rows, batch_rows = tokens.shape[0], grad_out.shape[0]
    core = lax.axis_index("core")

    grad_other = lax.ppermute(grad_out, "core", [(0, 1), (1, 0)])
    order = by_core(rank)
    projected = jnp.dot(tokens, basis, preferred_element_type=f32).astype(bf16)
    projected = jnp.dot(projected, order, preferred_element_type=f32).astype(bf16)
    sent = jnp.stack([projected[:, :half], projected[:, half:]])[:, None]
    sent = jnp.broadcast_to(sent, (2, tensor, own_rows, half))
    projected = lax.all_to_all(
        sent.reshape(2 * tensor, own_rows, half), ("core", "tensor"), 0, 0, tiled=True
    ).reshape(2 * batch_rows, half)
    contract = (((0,), (0,)), ((), ()))
    first = core == 0
    chip_sum = lax.dot_general(
        projected[:batch_rows], jnp.where(first, grad_out, grad_other), contract, preferred_element_type=f32
    ) + lax.dot_general(
        projected[batch_rows:], jnp.where(first, grad_other, grad_out), contract, preferred_element_type=f32
    )
    rows = lax.all_to_all(chip_sum.astype(bf16).reshape((half,) + piece), CHIPS, 0, 0, tiled=True)
    reduced = jnp.sum(rows.astype(f32), axis=0).reshape(1, columns)

    new_avg = 0.9 * exp_avg + 0.1 * reduced
    new_avg_sq = 0.999 * exp_avg_sq + 0.001 * reduced * reduced
    first_fix = 1.0 - 0.9**STEP
    second_fix = 1.0 - 0.999**STEP
    direction = (new_avg / first_fix / (jnp.sqrt(new_avg_sq / second_fix) + 1e-08)).astype(bf16)

    weight_rows = weight.shape[0]
    owner = lax.axis_index(("z", "x", "core"))
    basis_rows = lax.dynamic_slice_in_dim(basis, owner * weight_rows, weight_rows, 0)
    basis_rows = jnp.dot(basis_rows, order, preferred_element_type=f32).astype(bf16)
    direction, basis_rows = lax.optimization_barrier((direction, basis_rows))
    own_core = lax.all_to_all(
        jnp.broadcast_to(direction.reshape((1,) + piece), (half,) + piece), CHIPS, 0, 0, tiled=True
    )
    full = lax.all_gather(own_core, "core", axis=0, tiled=True).reshape(rank, columns)
    delta = jnp.dot(basis_rows, full, preferred_element_type=f32)
    return (weight - 0.5 * delta, new_avg, new_avg_sq)


def solution(mesh):
    split = Mesh(mesh.devices.reshape(8, 8, 2, 8), ("z", "x", "core", "tensor"))
    owners = ("z", "x", "core")
    shared = P(owners, "tensor")
    placed = (P(owners + ("tensor",), None), shared, P(), shared, shared, shared)
    return jax.shard_map(
        body, mesh=split, in_specs=placed, out_specs=(shared, shared, shared), check_vma=False
    )
```

```python
import functools

import jax
import jax.numpy as jnp
from jax import lax
from jax.experimental import pallas as pl
from jax.experimental.pallas import tpu as pltpu
from jax.sharding import Mesh
from jax.sharding import PartitionSpec as P

STEP = 10
CHIPS = ("z", "x")
VMEM_LIMIT = 16 * 1024 * 1024
TILE = 512


def chip_gradient(projected_ref, pick_ref, own_ref, other_ref, sum_ref, *, core_axis):
    batch = own_ref.shape[0]
    core = lax.axis_index(core_axis)
    own = projected_ref[pl.ds(pl.multiple_of(core * batch, batch), batch), :]
    other = projected_ref[pl.ds(pl.multiple_of((1 - core) * batch, batch), batch), :]
    contract = (((0,), (0,)), ((), ()))

    def ranks(rows):
        picked = lax.dot_general(
            pick_ref[...], rows, (((0,), (1,)), ((), ())), preferred_element_type=jnp.float32
        )
        return picked.astype(jnp.bfloat16)

    own, other = ranks(own), ranks(other)
    for start in range(0, own_ref.shape[1], TILE):
        cols = pl.ds(start, TILE)
        total = jnp.dot(own, own_ref[:, cols], preferred_element_type=jnp.float32)
        total = total + jnp.dot(other, other_ref[:, cols], preferred_element_type=jnp.float32)
        sum_ref[:, cols] = total.astype(jnp.bfloat16)


def moments(rows_ref, avg_ref, sq_ref, direction_ref, new_avg_ref, new_sq_ref):
    parts, width = rows_ref.shape[1:]
    reduced = jnp.sum(rows_ref[...].astype(jnp.float32), axis=0)
    pieces = [slice(i * width, (i + 1) * width) for i in range(parts)]
    avg = jnp.concatenate([avg_ref[:, p] for p in pieces], axis=0)
    sq = jnp.concatenate([sq_ref[:, p] for p in pieces], axis=0)
    new_avg = 0.9 * avg + 0.1 * reduced
    new_sq = 0.999 * sq + 0.001 * reduced * reduced
    first_fix = 1.0 - 0.9**STEP
    second_fix = 1.0 - 0.999**STEP
    direction = new_avg / first_fix / (jnp.sqrt(new_sq / second_fix) + 1e-08)
    direction_ref[...] = jnp.broadcast_to(direction.astype(jnp.bfloat16)[None], direction_ref.shape)
    for i, p in enumerate(pieces):
        new_avg_ref[:, p] = new_avg[i : i + 1]
        new_sq_ref[:, p] = new_sq[i : i + 1]


def body(tokens, grad_out, basis, weight, exp_avg, exp_avg_sq):
    f32, bf16 = jnp.float32, jnp.bfloat16
    rank, columns = basis.shape[1], grad_out.shape[1]
    half = rank // 2
    piece = (4, columns // 4)
    tensor = lax.axis_size("tensor")
    own_rows, batch_rows = tokens.shape[0], grad_out.shape[0]
    core = lax.axis_index("core")
    vmem = pl.BlockSpec(memory_space=pltpu.VMEM)
    params = pltpu.CompilerParams(vmem_limit_bytes=VMEM_LIMIT)

    row = lax.broadcasted_iota(jnp.int32, (rank, half), 0)
    column = lax.broadcasted_iota(jnp.int32, (rank, half), 1)
    pick = (row == 2 * column + core).astype(bf16)
    even, odd = (row == 2 * column).astype(bf16), (row == 2 * column + 1).astype(bf16)
    weight_rows = weight.shape[0]
    owner = lax.axis_index(("z", "x", "core"))
    basis_rows = lax.dynamic_slice_in_dim(basis, owner * weight_rows, weight_rows, 0)
    by_core = jnp.concatenate([even, odd], axis=1)
    basis_rows = jnp.dot(basis_rows, by_core, preferred_element_type=f32).astype(bf16)

    projected = jnp.dot(tokens, basis, preferred_element_type=f32).astype(bf16)
    projected, basis_rows, pick, grad_sent = lax.optimization_barrier((projected, basis_rows, pick, grad_out))
    grad_other = lax.ppermute(grad_sent, "core", [(0, 1), (1, 0)])
    projected = lax.all_to_all(
        jnp.broadcast_to(projected[None], (2 * tensor, own_rows, rank)), ("core", "tensor"), 0, 0, tiled=True
    ).reshape(2 * batch_rows, rank)
    in_vmem = functools.partial(pltpu.with_memory_space_constraint, memory_space=pltpu.VMEM)
    chip_sum = pl.pallas_call(
        functools.partial(chip_gradient, core_axis="core"),
        out_shape=pltpu.VMEM((half, columns), bf16),
        in_specs=[vmem] * 4,
        out_specs=vmem,
        compiler_params=params,
        name="chip_gradient",
    )(in_vmem(projected), in_vmem(pick), in_vmem(grad_out), in_vmem(grad_other))
    rows = lax.all_to_all(chip_sum.reshape((half,) + piece), CHIPS, 0, 0, tiled=True)
    direction, new_avg, new_avg_sq = pl.pallas_call(
        moments,
        out_shape=[
            pltpu.VMEM((half,) + piece, bf16),
            jax.ShapeDtypeStruct(exp_avg.shape, f32),
            jax.ShapeDtypeStruct(exp_avg.shape, f32),
        ],
        in_specs=[vmem] * 3,
        out_specs=[vmem] * 3,
        compiler_params=params,
        name="moments",
    )(in_vmem(rows), in_vmem(exp_avg), in_vmem(exp_avg_sq))

    own_core = lax.all_to_all(direction, CHIPS, 0, 0, tiled=True)
    full = lax.all_gather(own_core, "core", axis=0, tiled=True).reshape(rank, columns)
    delta = jnp.dot(basis_rows, full, preferred_element_type=f32)
    return (weight - 0.5 * delta, new_avg, new_avg_sq)


def solution(mesh):
    split = Mesh(mesh.devices.reshape(8, 8, 2, 8), ("z", "x", "core", "tensor"))
    owners = ("z", "x", "core")
    shared = P(owners, "tensor")
    placed = (P(owners + ("tensor",), None), shared, P(), shared, shared, shared)
    return jax.shard_map(
        body, mesh=split, in_specs=placed, out_specs=(shared, shared, shared), check_vma=False
    )
```

```python
import functools

import jax
import jax.numpy as jnp
from jax import lax
from jax.experimental import pallas as pl
from jax.experimental.pallas import tpu as pltpu
from jax.sharding import Mesh
from jax.sharding import PartitionSpec as P

STEP = 10
CHIPS = ("z", "x")
VMEM_LIMIT = 16 * 1024 * 1024
TILE = 512
PROJECT_PIECES = 2
OUT_PIECES = 4


def project(tokens_hbm, basis_hbm, sent_ref, rows_ref, tokens_ref, basis_ref, token_sems, basis_sems):
    depth = basis_ref.shape[0] // PROJECT_PIECES

    def copies(i):
        part = pl.ds(i * depth, depth)
        return (
            pltpu.make_async_copy(tokens_hbm.at[:, part], tokens_ref.at[:, part], token_sems.at[i]),
            pltpu.make_async_copy(basis_hbm.at[part, :], basis_ref.at[part, :], basis_sems.at[i]),
        )

    for i in range(PROJECT_PIECES):
        for copy in copies(i):
            copy.start()
    total = jnp.zeros((tokens_ref.shape[0], basis_ref.shape[1]), jnp.float32)
    for i in range(PROJECT_PIECES):
        for copy in copies(i):
            copy.wait()
        part = pl.ds(i * depth, depth)
        total = total + jnp.dot(
            tokens_ref[:, part], basis_ref[part, :], preferred_element_type=jnp.float32
        )
    sent_ref[...] = jnp.broadcast_to(total.astype(jnp.bfloat16)[None], sent_ref.shape)
    count, rank = rows_ref.shape
    half = rank // 2
    owner = lax.axis_index(("z", "x", "core"))
    row = lax.broadcasted_iota(jnp.int32, (rank, rank), 0)
    column = lax.broadcasted_iota(jnp.int32, (rank, rank), 1)
    wanted = jnp.where(column < half, 2 * column, 2 * (column - half) + 1)
    order = jnp.where(row == wanted, 1.0, 0.0).astype(jnp.bfloat16)
    rows = basis_ref[pl.ds(pl.multiple_of(owner * count, count), count), :]
    rows_ref[...] = jnp.dot(rows, order, preferred_element_type=jnp.float32).astype(jnp.bfloat16)


def update(rows_ref, direction_ref, weight_ref, new_hbm, new_ref, sems):
    width = weight_ref.shape[1] // OUT_PIECES
    out = []
    for i in range(OUT_PIECES):
        cols = pl.ds(i * width, width)
        delta = jnp.dot(rows_ref[...], direction_ref[:, cols], preferred_element_type=jnp.float32)
        new_ref[:, cols] = weight_ref[:, cols] - 0.5 * delta
        out.append(pltpu.make_async_copy(new_ref.at[:, cols], new_hbm.at[:, cols], sems.at[i]))
        out[-1].start()
    for copy in out:
        copy.wait()


def chip_gradient(projected_ref, own_ref, other_ref, sum_ref, *, core_axis):
    batch = own_ref.shape[0]
    core = lax.axis_index(core_axis)
    own = projected_ref[pl.ds(pl.multiple_of(core * batch, batch), batch), :]
    other = projected_ref[pl.ds(pl.multiple_of((1 - core) * batch, batch), batch), :]
    rank = projected_ref.shape[1]
    row = lax.broadcasted_iota(jnp.int32, (rank // 2, rank), 0)
    column = lax.broadcasted_iota(jnp.int32, (rank // 2, rank), 1)
    pick = jnp.where(column == 2 * row + core, 1.0, 0.0).astype(jnp.bfloat16)

    def ranks(rows):
        picked = lax.dot_general(
            pick, rows, (((1,), (1,)), ((), ())), preferred_element_type=jnp.float32
        )
        return picked.astype(jnp.bfloat16)

    own, other = ranks(own), ranks(other)
    for start in range(0, own_ref.shape[1], TILE):
        cols = pl.ds(start, TILE)
        total = jnp.dot(own, own_ref[:, cols], preferred_element_type=jnp.float32)
        total = total + jnp.dot(other, other_ref[:, cols], preferred_element_type=jnp.float32)
        sum_ref[:, cols] = total.astype(jnp.bfloat16)


def moments(rows_ref, avg_ref, sq_ref, direction_ref, new_avg_ref, new_sq_ref):
    parts, width = rows_ref.shape[1:]
    reduced = jnp.sum(rows_ref[...].astype(jnp.float32), axis=0)
    pieces = [slice(i * width, (i + 1) * width) for i in range(parts)]
    avg = jnp.concatenate([avg_ref[:, p] for p in pieces], axis=0)
    sq = jnp.concatenate([sq_ref[:, p] for p in pieces], axis=0)
    new_avg = 0.9 * avg + 0.1 * reduced
    new_sq = 0.999 * sq + 0.001 * reduced * reduced
    first_fix = 1.0 - 0.9**STEP
    second_fix = 1.0 - 0.999**STEP
    direction = new_avg / first_fix / (jnp.sqrt(new_sq / second_fix) + 1e-08)
    direction_ref[...] = jnp.broadcast_to(direction.astype(jnp.bfloat16)[None], direction_ref.shape)
    for i, p in enumerate(pieces):
        new_avg_ref[:, p] = new_avg[i : i + 1]
        new_sq_ref[:, p] = new_sq[i : i + 1]


def body(tokens, grad_out, basis, weight, exp_avg, exp_avg_sq):
    f32, bf16 = jnp.float32, jnp.bfloat16
    rank, columns = basis.shape[1], grad_out.shape[1]
    half = rank // 2
    piece = (4, columns // 4)
    tensor = lax.axis_size("tensor")
    own_rows, batch_rows = tokens.shape[0], grad_out.shape[0]
    vmem = pl.BlockSpec(memory_space=pltpu.VMEM)
    params = pltpu.CompilerParams(vmem_limit_bytes=VMEM_LIMIT)

    in_hbm = functools.partial(pltpu.with_memory_space_constraint, memory_space=pltpu.HBM)
    hbm = pl.BlockSpec(memory_space=pl.ANY)
    sent, basis_rows = pl.pallas_call(
        project,
        out_shape=[
            pltpu.VMEM((2 * tensor, own_rows, rank), bf16),
            pltpu.VMEM((weight.shape[0], rank), bf16),
        ],
        in_specs=[hbm] * 2,
        out_specs=[vmem] * 2,
        scratch_shapes=[
            pltpu.VMEM(tokens.shape, bf16),
            pltpu.VMEM(basis.shape, bf16),
            pltpu.SemaphoreType.DMA((PROJECT_PIECES,)),
            pltpu.SemaphoreType.DMA((PROJECT_PIECES,)),
        ],
        compiler_params=params,
        name="project",
    )(in_hbm(tokens), in_hbm(basis))
    projected = lax.all_to_all(sent, ("core", "tensor"), 0, 0, tiled=True).reshape(2 * batch_rows, rank)
    basis_rows, grad_sent = lax.optimization_barrier((basis_rows, grad_out))
    grad_other = lax.ppermute(grad_sent, "core", [(0, 1), (1, 0)])
    in_vmem = functools.partial(pltpu.with_memory_space_constraint, memory_space=pltpu.VMEM)
    chip_sum = pl.pallas_call(
        functools.partial(chip_gradient, core_axis="core"),
        out_shape=pltpu.VMEM((half, columns), bf16),
        in_specs=[vmem] * 3,
        out_specs=vmem,
        compiler_params=params,
        name="chip_gradient",
    )(in_vmem(projected), in_vmem(grad_out), in_vmem(grad_other))
    rows = lax.all_to_all(chip_sum.reshape((half,) + piece), CHIPS, 0, 0, tiled=True)
    direction, new_avg, new_avg_sq = pl.pallas_call(
        moments,
        out_shape=[
            pltpu.VMEM((half,) + piece, bf16),
            jax.ShapeDtypeStruct(exp_avg.shape, f32),
            jax.ShapeDtypeStruct(exp_avg.shape, f32),
        ],
        in_specs=[vmem] * 3,
        out_specs=[vmem] * 3,
        compiler_params=params,
        name="moments",
    )(in_vmem(rows), in_vmem(exp_avg), in_vmem(exp_avg_sq))

    own_core = lax.all_to_all(direction, CHIPS, 0, 0, tiled=True)
    full = lax.all_gather(own_core, "core", axis=0, tiled=True).reshape(rank, columns)
    new_weight = pl.pallas_call(
        update,
        out_shape=jax.ShapeDtypeStruct(weight.shape, f32),
        in_specs=[vmem] * 3,
        out_specs=hbm,
        scratch_shapes=[pltpu.VMEM(weight.shape, f32), pltpu.SemaphoreType.DMA((OUT_PIECES,))],
        compiler_params=params,
        name="update",
    )(in_vmem(basis_rows), in_vmem(full), in_vmem(weight))
    return (new_weight, new_avg, new_avg_sq)


def solution(mesh):
    split = Mesh(mesh.devices.reshape(8, 8, 2, 8), ("z", "x", "core", "tensor"))
    owners = ("z", "x", "core")
    shared = P(owners, "tensor")
    placed = (P(owners + ("tensor",), None), shared, P(), shared, shared, shared)
    return jax.shard_map(
        body, mesh=split, in_specs=placed, out_specs=(shared, shared, shared), check_vma=False
    )
```

```python
import functools

import jax
import jax.numpy as jnp
from jax import lax
from jax.experimental import pallas as pl
from jax.experimental.pallas import tpu as pltpu
from jax.sharding import Mesh
from jax.sharding import PartitionSpec as P

STEP = 10
CHIPS = ("z", "x")
VMEM_LIMIT = 16 * 1024 * 1024
TILE = 512
PROJECT_PIECES = 2
OUT_PIECES = 4


def project(tokens_hbm, basis_hbm, sent_ref, rows_ref, tokens_ref, basis_ref, token_sems, basis_sems):
    depth = basis_ref.shape[0] // PROJECT_PIECES

    def copies(i):
        part = pl.ds(i * depth, depth)
        return (
            pltpu.make_async_copy(tokens_hbm.at[:, part], tokens_ref.at[:, part], token_sems.at[i]),
            pltpu.make_async_copy(basis_hbm.at[part, :], basis_ref.at[part, :], basis_sems.at[i]),
        )

    for i in range(PROJECT_PIECES):
        for copy in copies(i):
            copy.start()
    total = jnp.zeros((tokens_ref.shape[0], basis_ref.shape[1]), jnp.float32)
    for i in range(PROJECT_PIECES):
        for copy in copies(i):
            copy.wait()
        part = pl.ds(i * depth, depth)
        total = total + jnp.dot(
            tokens_ref[:, part], basis_ref[part, :], preferred_element_type=jnp.float32
        )
    sent_ref[...] = jnp.broadcast_to(total.astype(jnp.bfloat16)[None], sent_ref.shape)
    count, rank = rows_ref.shape
    half = rank // 2
    owner = lax.axis_index(("z", "x", "core"))
    row = lax.broadcasted_iota(jnp.int32, (rank, rank), 0)
    column = lax.broadcasted_iota(jnp.int32, (rank, rank), 1)
    wanted = jnp.where(column < half, 2 * column, 2 * (column - half) + 1)
    order = jnp.where(row == wanted, 1.0, 0.0).astype(jnp.bfloat16)
    rows = basis_ref[pl.ds(pl.multiple_of(owner * count, count), count), :]
    rows_ref[...] = jnp.dot(rows, order, preferred_element_type=jnp.float32).astype(jnp.bfloat16)


def update(
    rows_ref, direction_ref, weight_ref, avg_ref, sq_ref, new_hbm, avg_hbm, sq_hbm, new_ref, sems, moment_sems
):
    out = [
        pltpu.make_async_copy(avg_ref, avg_hbm, moment_sems.at[0]),
        pltpu.make_async_copy(sq_ref, sq_hbm, moment_sems.at[1]),
    ]
    for copy in out:
        copy.start()
    width = weight_ref.shape[1] // OUT_PIECES
    for i in range(OUT_PIECES):
        cols = pl.ds(i * width, width)
        delta = jnp.dot(rows_ref[...], direction_ref[:, cols], preferred_element_type=jnp.float32)
        new_ref[:, cols] = weight_ref[:, cols] - 0.5 * delta
        out.append(pltpu.make_async_copy(new_ref.at[:, cols], new_hbm.at[:, cols], sems.at[i]))
        out[-1].start()
    for copy in out:
        copy.wait()


def chip_gradient(projected_ref, own_ref, other_ref, sum_ref, *, core_axis):
    batch = own_ref.shape[0]
    core = lax.axis_index(core_axis)
    own = projected_ref[pl.ds(pl.multiple_of(core * batch, batch), batch), :]
    other = projected_ref[pl.ds(pl.multiple_of((1 - core) * batch, batch), batch), :]
    rank = projected_ref.shape[1]
    row = lax.broadcasted_iota(jnp.int32, (rank // 2, rank), 0)
    column = lax.broadcasted_iota(jnp.int32, (rank // 2, rank), 1)
    pick = jnp.where(column == 2 * row + core, 1.0, 0.0).astype(jnp.bfloat16)

    def ranks(rows):
        picked = lax.dot_general(
            pick, rows, (((1,), (1,)), ((), ())), preferred_element_type=jnp.float32
        )
        return picked.astype(jnp.bfloat16)

    own, other = ranks(own), ranks(other)
    for start in range(0, own_ref.shape[1], TILE):
        cols = pl.ds(start, TILE)
        total = jnp.dot(own, own_ref[:, cols], preferred_element_type=jnp.float32)
        total = total + jnp.dot(other, other_ref[:, cols], preferred_element_type=jnp.float32)
        sum_ref[:, cols] = total.astype(jnp.bfloat16)


def moments(rows_ref, avg_ref, sq_ref, direction_ref, new_avg_ref, new_sq_ref):
    parts, width = rows_ref.shape[1:]
    reduced = jnp.sum(rows_ref[...].astype(jnp.float32), axis=0)
    pieces = [slice(i * width, (i + 1) * width) for i in range(parts)]
    avg = jnp.concatenate([avg_ref[:, p] for p in pieces], axis=0)
    sq = jnp.concatenate([sq_ref[:, p] for p in pieces], axis=0)
    new_avg = 0.9 * avg + 0.1 * reduced
    new_sq = 0.999 * sq + 0.001 * reduced * reduced
    first_fix = 1.0 - 0.9**STEP
    second_fix = 1.0 - 0.999**STEP
    direction = new_avg / first_fix / (jnp.sqrt(new_sq / second_fix) + 1e-08)
    direction_ref[...] = jnp.broadcast_to(direction.astype(jnp.bfloat16)[None], direction_ref.shape)
    for i, p in enumerate(pieces):
        new_avg_ref[:, p] = new_avg[i : i + 1]
        new_sq_ref[:, p] = new_sq[i : i + 1]


def body(tokens, grad_out, basis, weight, exp_avg, exp_avg_sq):
    f32, bf16 = jnp.float32, jnp.bfloat16
    rank, columns = basis.shape[1], grad_out.shape[1]
    half = rank // 2
    piece = (4, columns // 4)
    tensor = lax.axis_size("tensor")
    own_rows, batch_rows = tokens.shape[0], grad_out.shape[0]
    vmem = pl.BlockSpec(memory_space=pltpu.VMEM)
    params = pltpu.CompilerParams(vmem_limit_bytes=VMEM_LIMIT)

    in_hbm = functools.partial(pltpu.with_memory_space_constraint, memory_space=pltpu.HBM)
    hbm = pl.BlockSpec(memory_space=pl.ANY)
    sent, basis_rows = pl.pallas_call(
        project,
        out_shape=[
            pltpu.VMEM((2 * tensor, own_rows, rank), bf16),
            pltpu.VMEM((weight.shape[0], rank), bf16),
        ],
        in_specs=[hbm] * 2,
        out_specs=[vmem] * 2,
        scratch_shapes=[
            pltpu.VMEM(tokens.shape, bf16),
            pltpu.VMEM(basis.shape, bf16),
            pltpu.SemaphoreType.DMA((PROJECT_PIECES,)),
            pltpu.SemaphoreType.DMA((PROJECT_PIECES,)),
        ],
        compiler_params=params,
        name="project",
    )(in_hbm(tokens), in_hbm(basis))
    projected = lax.all_to_all(sent, ("core", "tensor"), 0, 0, tiled=True).reshape(2 * batch_rows, rank)
    basis_rows, grad_sent = lax.optimization_barrier((basis_rows, grad_out))
    grad_other = lax.ppermute(grad_sent, "core", [(0, 1), (1, 0)])
    in_vmem = functools.partial(pltpu.with_memory_space_constraint, memory_space=pltpu.VMEM)
    chip_sum = pl.pallas_call(
        functools.partial(chip_gradient, core_axis="core"),
        out_shape=pltpu.VMEM((half, columns), bf16),
        in_specs=[vmem] * 3,
        out_specs=vmem,
        compiler_params=params,
        name="chip_gradient",
    )(in_vmem(projected), in_vmem(grad_out), in_vmem(grad_other))
    rows = lax.all_to_all(chip_sum.reshape((half,) + piece), CHIPS, 0, 0, tiled=True)
    direction, new_avg, new_avg_sq = pl.pallas_call(
        moments,
        out_shape=[
            pltpu.VMEM((half,) + piece, bf16),
            pltpu.VMEM(exp_avg.shape, f32),
            pltpu.VMEM(exp_avg.shape, f32),
        ],
        in_specs=[vmem] * 3,
        out_specs=[vmem] * 3,
        compiler_params=params,
        name="moments",
    )(in_vmem(rows), in_vmem(exp_avg), in_vmem(exp_avg_sq))

    own_core = lax.all_to_all(direction, CHIPS, 0, 0, tiled=True)
    full = lax.all_gather(own_core, "core", axis=0, tiled=True).reshape(rank, columns)
    return pl.pallas_call(
        update,
        out_shape=[jax.ShapeDtypeStruct(array.shape, f32) for array in (weight, exp_avg, exp_avg_sq)],
        in_specs=[vmem] * 5,
        out_specs=[hbm] * 3,
        scratch_shapes=[
            pltpu.VMEM(weight.shape, f32),
            pltpu.SemaphoreType.DMA((OUT_PIECES,)),
            pltpu.SemaphoreType.DMA((2,)),
        ],
        compiler_params=params,
        name="update",
    )(in_vmem(basis_rows), in_vmem(full), in_vmem(weight), in_vmem(new_avg), in_vmem(new_avg_sq))


def solution(mesh):
    split = Mesh(mesh.devices.reshape(8, 8, 2, 8), ("z", "x", "core", "tensor"))
    owners = ("z", "x", "core")
    shared = P(owners, "tensor")
    placed = (P(owners + ("tensor",), None), shared, P(), shared, shared, shared)
    return jax.shard_map(
        body, mesh=split, in_specs=placed, out_specs=(shared, shared, shared), check_vma=False
    )
```

```python
import functools

import jax
import jax.numpy as jnp
from jax import lax
from jax.experimental import pallas as pl
from jax.experimental.pallas import tpu as pltpu
from jax.sharding import Mesh
from jax.sharding import PartitionSpec as P

STEP = 10
CHIPS = ("z", "x")
VMEM_LIMIT = 16 * 1024 * 1024
TILE = 512
PROJECT_PIECES = 2
OUT_PIECES = 4


def project(tokens_hbm, basis_hbm, sent_ref, rows_ref, tokens_ref, basis_ref, token_sems, basis_sems):
    depth = basis_ref.shape[0] // PROJECT_PIECES

    def copies(i):
        part = pl.ds(i * depth, depth)
        return (
            pltpu.make_async_copy(tokens_hbm.at[:, part], tokens_ref.at[:, part], token_sems.at[i]),
            pltpu.make_async_copy(basis_hbm.at[part, :], basis_ref.at[part, :], basis_sems.at[i]),
        )

    for i in range(PROJECT_PIECES):
        for copy in copies(i):
            copy.start()
    total = jnp.zeros((tokens_ref.shape[0], basis_ref.shape[1]), jnp.float32)
    for i in range(PROJECT_PIECES):
        for copy in copies(i):
            copy.wait()
        part = pl.ds(i * depth, depth)
        total = total + jnp.dot(
            tokens_ref[:, part], basis_ref[part, :], preferred_element_type=jnp.float32
        )
    sent_ref[...] = jnp.broadcast_to(total.astype(jnp.bfloat16)[None], sent_ref.shape)
    count = rows_ref.shape[0]
    owner = lax.axis_index(("z", "x", "core"))
    rows_ref[...] = basis_ref[pl.ds(pl.multiple_of(owner * count, count), count), :]


def update(
    rows_ref, direction_ref, weight_ref, avg_ref, sq_ref, new_hbm, avg_hbm, sq_hbm, new_ref, sems, moment_sems
):
    out = [
        pltpu.make_async_copy(avg_ref, avg_hbm, moment_sems.at[0]),
        pltpu.make_async_copy(sq_ref, sq_hbm, moment_sems.at[1]),
    ]
    for copy in out:
        copy.start()
    width = weight_ref.shape[1] // OUT_PIECES
    for i in range(OUT_PIECES):
        cols = pl.ds(i * width, width)
        delta = jnp.dot(rows_ref[...], direction_ref[:, cols], preferred_element_type=jnp.float32)
        new_ref[:, cols] = weight_ref[:, cols] - 0.5 * delta
        out.append(pltpu.make_async_copy(new_ref.at[:, cols], new_hbm.at[:, cols], sems.at[i]))
        out[-1].start()
    for copy in out:
        copy.wait()


def chip_gradient(projected_ref, own_ref, other_ref, sum_ref, *, core_axis):
    batch = own_ref.shape[0]
    core = lax.axis_index(core_axis)
    own = projected_ref[pl.ds(pl.multiple_of(core * batch, batch), batch), :]
    other = projected_ref[pl.ds(pl.multiple_of((1 - core) * batch, batch), batch), :]
    rank = projected_ref.shape[1]
    row = lax.broadcasted_iota(jnp.int32, (rank // 2, rank), 0)
    column = lax.broadcasted_iota(jnp.int32, (rank // 2, rank), 1)
    pick = jnp.where(column == 2 * row + core, 1.0, 0.0).astype(jnp.bfloat16)

    def ranks(rows):
        picked = lax.dot_general(
            pick, rows, (((1,), (1,)), ((), ())), preferred_element_type=jnp.float32
        )
        return picked.astype(jnp.bfloat16)

    own, other = ranks(own), ranks(other)
    for start in range(0, own_ref.shape[1], TILE):
        cols = pl.ds(start, TILE)
        total = jnp.dot(own, own_ref[:, cols], preferred_element_type=jnp.float32)
        total = total + jnp.dot(other, other_ref[:, cols], preferred_element_type=jnp.float32)
        sum_ref[:, cols] = total.astype(jnp.bfloat16)


def moments(rows_ref, avg_ref, sq_ref, direction_ref, new_avg_ref, new_sq_ref):
    parts, width = rows_ref.shape[1:]
    reduced = jnp.sum(rows_ref[...].astype(jnp.float32), axis=0)
    pieces = [slice(i * width, (i + 1) * width) for i in range(parts)]
    avg = jnp.concatenate([avg_ref[:, p] for p in pieces], axis=0)
    sq = jnp.concatenate([sq_ref[:, p] for p in pieces], axis=0)
    new_avg = 0.9 * avg + 0.1 * reduced
    new_sq = 0.999 * sq + 0.001 * reduced * reduced
    first_fix = 1.0 - 0.9**STEP
    second_fix = 1.0 - 0.999**STEP
    direction = new_avg / first_fix / (jnp.sqrt(new_sq / second_fix) + 1e-08)
    direction_ref[...] = jnp.broadcast_to(direction.astype(jnp.bfloat16)[None], direction_ref.shape)
    for i, p in enumerate(pieces):
        new_avg_ref[:, p] = new_avg[i : i + 1]
        new_sq_ref[:, p] = new_sq[i : i + 1]


def body(tokens, grad_out, basis, weight, exp_avg, exp_avg_sq):
    f32, bf16 = jnp.float32, jnp.bfloat16
    rank, columns = basis.shape[1], grad_out.shape[1]
    half = rank // 2
    piece = (4, columns // 4)
    tensor = lax.axis_size("tensor")
    own_rows, batch_rows = tokens.shape[0], grad_out.shape[0]
    vmem = pl.BlockSpec(memory_space=pltpu.VMEM)
    params = pltpu.CompilerParams(vmem_limit_bytes=VMEM_LIMIT)

    in_hbm = functools.partial(pltpu.with_memory_space_constraint, memory_space=pltpu.HBM)
    hbm = pl.BlockSpec(memory_space=pl.ANY)
    sent, basis_rows = pl.pallas_call(
        project,
        out_shape=[
            jax.ShapeDtypeStruct((2 * tensor, own_rows, rank), bf16),
            pltpu.VMEM((weight.shape[0], rank), bf16),
        ],
        in_specs=[hbm] * 2,
        out_specs=[vmem] * 2,
        scratch_shapes=[
            pltpu.VMEM(tokens.shape, bf16),
            pltpu.VMEM(basis.shape, bf16),
            pltpu.SemaphoreType.DMA((PROJECT_PIECES,)),
            pltpu.SemaphoreType.DMA((PROJECT_PIECES,)),
        ],
        compiler_params=params,
        name="project",
    )(in_hbm(tokens), in_hbm(basis))
    projected = lax.all_to_all(sent, ("core", "tensor"), 0, 0, tiled=True).reshape(2 * batch_rows, rank)
    row = lax.broadcasted_iota(jnp.int32, (half, rank), 0)
    column = lax.broadcasted_iota(jnp.int32, (half, rank), 1)
    order = jnp.concatenate([column == 2 * row, column == 2 * row + 1]).astype(bf16)
    basis_rows = lax.dot_general(
        basis_rows, order, (((1,), (1,)), ((), ())), preferred_element_type=f32
    ).astype(bf16)
    grad_sent = lax.optimization_barrier((sent, grad_out))[1]
    grad_other = jnp.concatenate(
        [lax.ppermute(part, "core", [(0, 1), (1, 0)]) for part in jnp.split(grad_sent, 2)]
    )
    projected, basis_rows = lax.optimization_barrier((projected, basis_rows))
    in_vmem = functools.partial(pltpu.with_memory_space_constraint, memory_space=pltpu.VMEM)
    chip_sum = pl.pallas_call(
        functools.partial(chip_gradient, core_axis="core"),
        out_shape=pltpu.VMEM((half, columns), bf16),
        in_specs=[vmem] * 3,
        out_specs=vmem,
        compiler_params=params,
        name="chip_gradient",
    )(in_vmem(projected), in_vmem(grad_out), in_vmem(grad_other))
    rows = lax.all_to_all(chip_sum.reshape((half,) + piece), CHIPS, 0, 0, tiled=True)
    direction, new_avg, new_avg_sq = pl.pallas_call(
        moments,
        out_shape=[
            pltpu.VMEM((half,) + piece, bf16),
            pltpu.VMEM(exp_avg.shape, f32),
            pltpu.VMEM(exp_avg.shape, f32),
        ],
        in_specs=[vmem] * 3,
        out_specs=[vmem] * 3,
        compiler_params=params,
        name="moments",
    )(in_vmem(rows), in_vmem(exp_avg), in_vmem(exp_avg_sq))

    own_core = lax.all_to_all(direction, CHIPS, 0, 0, tiled=True)
    full = lax.all_gather(own_core, "core", axis=0, tiled=True).reshape(rank, columns)
    return pl.pallas_call(
        update,
        out_shape=[jax.ShapeDtypeStruct(array.shape, f32) for array in (weight, exp_avg, exp_avg_sq)],
        in_specs=[vmem] * 5,
        out_specs=[hbm] * 3,
        scratch_shapes=[
            pltpu.VMEM(weight.shape, f32),
            pltpu.SemaphoreType.DMA((OUT_PIECES,)),
            pltpu.SemaphoreType.DMA((2,)),
        ],
        compiler_params=params,
        name="update",
    )(in_vmem(basis_rows), in_vmem(full), in_vmem(weight), in_vmem(new_avg), in_vmem(new_avg_sq))


def solution(mesh):
    split = Mesh(mesh.devices.reshape(8, 8, 2, 8), ("z", "x", "core", "tensor"))
    owners = ("z", "x", "core")
    shared = P(owners, "tensor")
    placed = (P(owners + ("tensor",), None), shared, P(), shared, shared, shared)
    return jax.shard_map(
        body, mesh=split, in_specs=placed, out_specs=(shared, shared, shared), check_vma=False
    )
```

```python
import functools

import jax
import jax.numpy as jnp
from jax import lax
from jax.experimental import pallas as pl
from jax.experimental.pallas import tpu as pltpu
from jax.sharding import Mesh
from jax.sharding import PartitionSpec as P

STEP = 10
CHIPS = ("z", "x")
VMEM_LIMIT = 16 * 1024 * 1024
TILE = 512
PROJECT_PIECES = 2
OUT_PIECES = 4


def project(tokens_hbm, basis_hbm, sent_ref, rows_ref, tokens_ref, basis_ref, token_sems, basis_sems):
    depth = basis_ref.shape[0] // PROJECT_PIECES

    def copies(i):
        part = pl.ds(i * depth, depth)
        return (
            pltpu.make_async_copy(tokens_hbm.at[:, part], tokens_ref.at[:, part], token_sems.at[i]),
            pltpu.make_async_copy(basis_hbm.at[part, :], basis_ref.at[part, :], basis_sems.at[i]),
        )

    for i in range(PROJECT_PIECES):
        for copy in copies(i):
            copy.start()
    total = jnp.zeros((tokens_ref.shape[0], basis_ref.shape[1]), jnp.float32)
    for i in range(PROJECT_PIECES):
        for copy in copies(i):
            copy.wait()
        part = pl.ds(i * depth, depth)
        total = total + jnp.dot(
            tokens_ref[:, part], basis_ref[part, :], preferred_element_type=jnp.float32
        )
    sent_ref[...] = jnp.broadcast_to(total.astype(jnp.bfloat16)[None], sent_ref.shape)
    count = rows_ref.shape[0]
    owner = lax.axis_index(("z", "x", "core"))
    rows_ref[...] = basis_ref[pl.ds(pl.multiple_of(owner * count, count), count), :]


def update(
    rows_ref, direction_ref, weight_ref, avg_ref, sq_ref, new_hbm, avg_hbm, sq_hbm, new_ref, sems, moment_sems
):
    out = [
        pltpu.make_async_copy(avg_ref, avg_hbm, moment_sems.at[0]),
        pltpu.make_async_copy(sq_ref, sq_hbm, moment_sems.at[1]),
    ]
    for copy in out:
        copy.start()
    width = weight_ref.shape[1] // OUT_PIECES
    for i in range(OUT_PIECES):
        cols = pl.ds(i * width, width)
        delta = jnp.dot(rows_ref[...], direction_ref[:, cols], preferred_element_type=jnp.float32)
        new_ref[:, cols] = weight_ref[:, cols] - 0.5 * delta
        out.append(pltpu.make_async_copy(new_ref.at[:, cols], new_hbm.at[:, cols], sems.at[i]))
        out[-1].start()
    for copy in out:
        copy.wait()


def own_gradient(projected_ref, own_ref, own_sum_ref, others_ref, *, core_axis):
    batch, part = own_ref.shape[0], others_ref.shape[2]
    core = lax.axis_index(core_axis)
    rank = projected_ref.shape[1]
    row = lax.broadcasted_iota(jnp.int32, (rank // 2, rank), 0)
    column = lax.broadcasted_iota(jnp.int32, (rank // 2, rank), 1)
    pick = jnp.where(column == 2 * row + core, 1.0, 0.0).astype(jnp.bfloat16)

    def ranks(start, count):
        rows = projected_ref[pl.ds(pl.multiple_of(start, count), count), :]
        picked = lax.dot_general(pick, rows, (((1,), (1,)), ((), ())), preferred_element_type=jnp.float32)
        return picked.astype(jnp.bfloat16)

    own = ranks(core * batch, batch)
    for i in range(others_ref.shape[0]):
        others_ref[i] = ranks((1 - core) * batch + i * part, part)
    for start in range(0, own_ref.shape[1], TILE):
        cols = pl.ds(start, TILE)
        own_sum_ref[:, cols] = jnp.dot(own, own_ref[:, cols], preferred_element_type=jnp.float32)


def add_other(own_sum_ref, others_ref, head_ref, tail_ref, sum_ref):
    for start in range(0, head_ref.shape[1], TILE):
        cols = pl.ds(start, TILE)
        total = own_sum_ref[:, cols]
        total = total + jnp.dot(others_ref[0], head_ref[:, cols], preferred_element_type=jnp.float32)
        total = total + jnp.dot(others_ref[1], tail_ref[:, cols], preferred_element_type=jnp.float32)
        sum_ref[:, cols] = total.astype(jnp.bfloat16)


def moments(rows_ref, avg_ref, sq_ref, direction_ref, new_avg_ref, new_sq_ref):
    parts, width = rows_ref.shape[1:]
    reduced = jnp.sum(rows_ref[...].astype(jnp.float32), axis=0)
    pieces = [slice(i * width, (i + 1) * width) for i in range(parts)]
    avg = jnp.concatenate([avg_ref[:, p] for p in pieces], axis=0)
    sq = jnp.concatenate([sq_ref[:, p] for p in pieces], axis=0)
    new_avg = 0.9 * avg + 0.1 * reduced
    new_sq = 0.999 * sq + 0.001 * reduced * reduced
    first_fix = 1.0 - 0.9**STEP
    second_fix = 1.0 - 0.999**STEP
    direction = new_avg / first_fix / (jnp.sqrt(new_sq / second_fix) + 1e-08)
    direction_ref[...] = jnp.broadcast_to(direction.astype(jnp.bfloat16)[None], direction_ref.shape)
    for i, p in enumerate(pieces):
        new_avg_ref[:, p] = new_avg[i : i + 1]
        new_sq_ref[:, p] = new_sq[i : i + 1]


def body(tokens, grad_out, basis, weight, exp_avg, exp_avg_sq):
    f32, bf16 = jnp.float32, jnp.bfloat16
    rank, columns = basis.shape[1], grad_out.shape[1]
    half = rank // 2
    piece = (4, columns // 4)
    tensor = lax.axis_size("tensor")
    own_rows, batch_rows = tokens.shape[0], grad_out.shape[0]
    vmem = pl.BlockSpec(memory_space=pltpu.VMEM)
    params = pltpu.CompilerParams(vmem_limit_bytes=VMEM_LIMIT)

    in_hbm = functools.partial(pltpu.with_memory_space_constraint, memory_space=pltpu.HBM)
    hbm = pl.BlockSpec(memory_space=pl.ANY)
    sent, basis_rows = pl.pallas_call(
        project,
        out_shape=[
            jax.ShapeDtypeStruct((2 * tensor, own_rows, rank), bf16),
            pltpu.VMEM((weight.shape[0], rank), bf16),
        ],
        in_specs=[hbm] * 2,
        out_specs=[vmem] * 2,
        scratch_shapes=[
            pltpu.VMEM(tokens.shape, bf16),
            pltpu.VMEM(basis.shape, bf16),
            pltpu.SemaphoreType.DMA((PROJECT_PIECES,)),
            pltpu.SemaphoreType.DMA((PROJECT_PIECES,)),
        ],
        compiler_params=params,
        name="project",
    )(in_hbm(tokens), in_hbm(basis))
    projected = lax.all_to_all(sent, ("core", "tensor"), 0, 0, tiled=True).reshape(2 * batch_rows, rank)
    row = lax.broadcasted_iota(jnp.int32, (half, rank), 0)
    column = lax.broadcasted_iota(jnp.int32, (half, rank), 1)
    order = jnp.concatenate([column == 2 * row, column == 2 * row + 1]).astype(bf16)
    basis_rows = lax.dot_general(
        basis_rows, order, (((1,), (1,)), ((), ())), preferred_element_type=f32
    ).astype(bf16)
    grad_sent = lax.optimization_barrier((sent, grad_out))[1]
    head, tail = [lax.ppermute(part, "core", [(0, 1), (1, 0)]) for part in jnp.split(grad_sent, 2)]
    projected, basis_rows = lax.optimization_barrier((projected, basis_rows))
    in_vmem = functools.partial(pltpu.with_memory_space_constraint, memory_space=pltpu.VMEM)
    own_sum, others = pl.pallas_call(
        functools.partial(own_gradient, core_axis="core"),
        out_shape=[pltpu.VMEM((half, columns), f32), pltpu.VMEM((2, half, batch_rows // 2), bf16)],
        in_specs=[vmem] * 2,
        out_specs=[vmem] * 2,
        compiler_params=params,
        name="own_gradient",
    )(in_vmem(projected), in_vmem(grad_out))
    chip_sum = pl.pallas_call(
        add_other,
        out_shape=pltpu.VMEM((half, columns), bf16),
        in_specs=[vmem] * 4,
        out_specs=vmem,
        compiler_params=params,
        name="add_other",
    )(in_vmem(own_sum), in_vmem(others), in_vmem(head), in_vmem(tail))
    rows = lax.all_to_all(chip_sum.reshape((half,) + piece), CHIPS, 0, 0, tiled=True)
    direction, new_avg, new_avg_sq = pl.pallas_call(
        moments,
        out_shape=[
            pltpu.VMEM((half,) + piece, bf16),
            pltpu.VMEM(exp_avg.shape, f32),
            pltpu.VMEM(exp_avg.shape, f32),
        ],
        in_specs=[vmem] * 3,
        out_specs=[vmem] * 3,
        compiler_params=params,
        name="moments",
    )(in_vmem(rows), in_vmem(exp_avg), in_vmem(exp_avg_sq))

    own_core = lax.all_to_all(direction, CHIPS, 0, 0, tiled=True)
    full = lax.all_gather(own_core, "core", axis=0, tiled=True).reshape(rank, columns)
    return pl.pallas_call(
        update,
        out_shape=[jax.ShapeDtypeStruct(array.shape, f32) for array in (weight, exp_avg, exp_avg_sq)],
        in_specs=[vmem] * 5,
        out_specs=[hbm] * 3,
        scratch_shapes=[
            pltpu.VMEM(weight.shape, f32),
            pltpu.SemaphoreType.DMA((OUT_PIECES,)),
            pltpu.SemaphoreType.DMA((2,)),
        ],
        compiler_params=params,
        name="update",
    )(in_vmem(basis_rows), in_vmem(full), in_vmem(weight), in_vmem(new_avg), in_vmem(new_avg_sq))


def solution(mesh):
    split = Mesh(mesh.devices.reshape(8, 8, 2, 8), ("z", "x", "core", "tensor"))
    owners = ("z", "x", "core")
    shared = P(owners, "tensor")
    placed = (P(owners + ("tensor",), None), shared, P(), shared, shared, shared)
    return jax.shard_map(
        body, mesh=split, in_specs=placed, out_specs=(shared, shared, shared), check_vma=False
    )
```
